32 devices in a mesh: ty: 8 (over y, x, core), tx: 4 (over z).
Axes of the slice: x: 2, y: 2, z: 4, core: 2. Of those that a mesh axis runs over, the one named last changes fastest.
Arguments:
- specimen: float32 [2, 4096, 2048], P(None, 'ty', 'tx'), may hold values from -6 to 6
- probe_field: float32 [2, 256, 256], replicated, may hold values from -6 to 6
- intensity: float32 [256, 256, 256], P(('ty', 'tx')), may hold values from 0.05 to 4
- positions: int32 [256, 2], P(('ty', 'tx')), may hold values from 0 to 3840, as said below
- occupied_slots: int32 [256], P(('ty', 'tx')), may hold values from 0 to 1, as said below
Outputs:
- new_specimen: float32 [2, 4096, 2048], P(None, 'ty', 'tx')
- new_probe: float32 [2, 256, 256], replicated
The draws below stay inside these ranges and needn't reach their ends.
Inputs may be any that keep to these rules, and one draw needn't show every extreme that they name: `positions`: slots are grouped by tile, 8 to a tile, tiles in the order of ty then tx. A slot of tile (a, b) has its row between a * 512 - 256 // 2 and a * 512 + 512 - 256 // 2 and its column between b * 512 - 256 // 2 and b * 512 + 512 - 256 // 2, and its window lies inside the object. `occupied_slots`: on each tile the live slots come first; each tile has 1 to 8 live slots, and some tile has all 8.
All inputs are finite; a program needn't handle non-finite values.
Results may differ from the reference program's by a relative error of at most 0.0003.
Values sent between devices are 32-bit elements; how exact they have to be, the bound alone decides.
A program may use at most 192 MiB of HBM per device.

```python
import math
import jax
import jax.numpy as jnp
from jax import lax

W = 256
TILE = 512
PMAX = 8
ITERS = 2
NR = 4096
NC = 2048
POS_ALL = 256


def slot_counts(key):
    tile_total = POS_ALL // PMAX
    base_key = jax.random.fold_in(key, 7103)
    key_base, key_full, key_pick = jax.random.split(base_key, 3)
    base = jax.random.randint(key_base, (tile_total,), 1, 5)
    full = jax.random.randint(key_full, (tile_total,), 0, 8) == 0
    chosen = jax.random.randint(key_pick, (), 0, tile_total)
    counts = jnp.where(full | (jnp.arange(tile_total) == chosen), PMAX, base)
    return jnp.minimum(counts, PMAX)


def draw_occupied_slots(key, part):
    counts = slot_counts(key)
    slot_index = jnp.arange(PMAX)
    return (slot_index[None, :] < counts[:, None]).astype(jnp.int32).reshape(POS_ALL)


def draw_positions(key, part):
    columns_of = NC // TILE
    tile_index = jnp.arange(POS_ALL) // PMAX
    tile_row = tile_index // columns_of
    tile_col = tile_index % columns_of
    key_row, key_col = jax.random.split(jax.random.fold_in(key, 9241))
    margin = W // 2
    rows = tile_row * TILE - margin + jax.random.randint(key_row, (POS_ALL,), 0, TILE + 1)
    cols = tile_col * TILE - margin + jax.random.randint(key_col, (POS_ALL,), 0, TILE + 1)
    rows = jnp.clip(rows, 0, NR - W)
    cols = jnp.clip(cols, 0, NC - W)
    last_first = POS_ALL - PMAX
    rows = rows.at[0].set(0).at[last_first].set(NR - W)
    cols = cols.at[0].set(0).at[last_first].set(NC - W)
    return jnp.stack([rows, cols], axis=1).astype(jnp.int32)


def block_levels(rng, extent, shards, smallest, top_value):
    gain = 1.0
    for dim, blocks in shards:
        draws = jax.random.uniform(jax.random.fold_in(jax.random.fold_in(rng, 6), dim), (blocks,), jnp.float32, smallest / len(shards), top_value / len(shards))
        gain = gain * jnp.repeat(jnp.exp(draws), extent[dim] // blocks).reshape((-1,) + (1,) * (len(extent) - 1 - dim))
    return gain


def centred(own_key, shape, width, most, pieces=(), kind=jnp.bfloat16):
    result = width * jax.random.normal(own_key, shape, jnp.float32)
    if pieces:
        result = result * block_levels(own_key, shape, pieces, -0.22, 0.18)
    return jnp.clip(result, -most, most).astype(kind)


def setup_inputs(seed: int = 0) -> dict:
    key_list = jax.random.split(jax.random.key(seed), 6)
    return {
        "specimen": centred(key_list[0], (2, NR, NC), 1.0, 6.0, ((1, 8), (2, 4)), jnp.float32),
        "probe_field": centred(key_list[1], (2, W, W), 1.0, 6.0, (), jnp.float32),
        "intensity": jnp.clip(jnp.exp(math.log(4.0) - 4.3820266 * jax.random.uniform(key_list[2], (POS_ALL, W, W), jnp.float32) ** block_levels(key_list[2], (POS_ALL, W, W), ((0, 32),), -0.2, 0.2)), 0.05, 4.0),
        "positions": draw_positions(jax.random.fold_in(key_list[5], 71), 0),
        "occupied_slots": draw_occupied_slots(jax.random.fold_in(key_list[5], 71), 0),
    }


FLOOR = 0.2
SPECIMEN_REG = 0.5
PROBE_REG = 1.0

def single_sweep(specimen, probe_field, positions, measured_amplitude, slot_occupancy):
    probe_real = probe_field[0]
    probe_imag = probe_field[1]
    anchor = jnp.zeros((), jnp.int32)

    def visit_position(state_tuple, inputs):
        totals, grad_real, grad_imag, density = state_tuple
        corner, measured, weight_live = inputs
        start_row = corner[0].astype(jnp.int32)
        start_col = corner[1].astype(jnp.int32)
        patch = lax.dynamic_slice(specimen, (anchor, start_row, start_col), (2, W, W))
        patch_real = patch[0]
        patch_imag = patch[1]
        exit_real = probe_real * patch_real - probe_imag * patch_imag
        exit_imag = probe_real * patch_imag + probe_imag * patch_real
        spectrum = jnp.fft.fft2(lax.complex(exit_real, exit_imag), norm='ortho')
        spectrum_real = jnp.real(spectrum)
        spectrum_imag = jnp.imag(spectrum)
        magnitude = jnp.sqrt(spectrum_real * spectrum_real + spectrum_imag * spectrum_imag)
        factor = measured / jnp.maximum(magnitude, FLOOR)
        back = jnp.fft.ifft2(lax.complex(spectrum_real * factor, spectrum_imag * factor), norm='ortho')
        diff_real = weight_live * (jnp.real(back) - exit_real)
        diff_imag = weight_live * (jnp.imag(back) - exit_imag)
        contribution = jnp.stack([probe_real * diff_real + probe_imag * diff_imag, probe_real * diff_imag - probe_imag * diff_real, weight_live * (probe_real * probe_real + probe_imag * probe_imag)])
        region = lax.dynamic_slice(totals, (anchor, start_row, start_col), (3, W, W))
        totals = lax.dynamic_update_slice(totals, region + contribution, (anchor, start_row, start_col))
        grad_real = grad_real + patch_real * diff_real + patch_imag * diff_imag
        grad_imag = grad_imag + patch_real * diff_imag - patch_imag * diff_real
        density = density + weight_live * (patch_real * patch_real + patch_imag * patch_imag)
        return ((totals, grad_real, grad_imag, density), None)
    starting_state = (jnp.zeros((3,) + specimen.shape[1:], specimen.dtype), jnp.zeros(probe_real.shape, specimen.dtype), jnp.zeros(probe_real.shape, specimen.dtype), jnp.zeros(probe_real.shape, specimen.dtype))
    converged_state, unused_value = lax.scan(visit_position, starting_state, (positions, measured_amplitude, slot_occupancy))
    totals, grad_real, grad_imag, density = converged_state
    new_specimen = specimen + totals[:2] / (totals[2] + SPECIMEN_REG)
    new_probe = probe_field + jnp.stack([grad_real, grad_imag]) / (density + PROBE_REG)
    return (new_specimen, new_probe)

def reference(specimen, probe_field, intensity, positions, occupied_slots):
    measured_amplitude = jnp.sqrt(intensity)
    slot_occupancy = occupied_slots.astype(specimen.dtype)
    for iteration in range(ITERS):
        specimen, probe_field = single_sweep(specimen, probe_field, positions, measured_amplitude, slot_occupancy)
    return (specimen, probe_field)
```

```python
import functools
import math

import jax
import jax.numpy as jnp
import ml_dtypes
import numpy as np
from jax import lax
from jax.experimental import pallas as pl
from jax.experimental.pallas import tpu as pltpu
from jax.sharding import PartitionSpec as P

ITERS = 2


FLOOR = 0.2
SPECIMEN_REG = 0.5
PROBE_REG = 1.0
LANES = 128
SUBLANES = 8


def split_np(table):
    hi = table.astype(ml_dtypes.bfloat16)
    lo = (table - hi.astype(np.float64)).astype(ml_dtypes.bfloat16)
    return hi, lo


def tables(window):
    half = window // 2
    j = np.arange(half)[:, None]
    m = np.arange(window)[None, :]
    angle = 2.0 * math.pi * ((j * m) % window) / window
    lower = np.sin(angle)
    lower[0] = np.cos(math.pi * m[0])
    real_dft = np.concatenate([np.cos(angle), lower]) / math.sqrt(window)
    hi, lo = split_np(real_dft)
    wide = np.concatenate([hi, hi, lo], axis=1)
    hi_t, lo_t = hi.T.copy(), lo.T.copy()
    wide_t = np.concatenate([hi_t, hi_t, lo_t], axis=1)
    order = np.concatenate([np.arange(half + 1), np.arange(window - 1, half, -1)])
    perm = np.zeros((window, window), ml_dtypes.bfloat16)
    perm[np.arange(window), order] = 1
    return (
        wide,
        wide.T.copy(),
        wide_t,
        wide_t.T.copy(),
        perm,
        perm.T.copy(),
    )


def dot(a, b):
    return jnp.dot(a, b, preferred_element_type=jnp.float32)


def split(x):
    hi = x.astype(jnp.bfloat16)
    return hi, (x - hi.astype(jnp.float32)).astype(jnp.bfloat16)


def times_left(wide, x):
    hi, lo = split(x)
    return dot(wide, jnp.concatenate([hi, lo, hi], axis=0))


def times_right(x, wide):
    hi, lo = split(x)
    return dot(jnp.concatenate([hi, lo, hi], axis=1), wide)


def halves(x, axis):
    half = x.shape[axis] // 2
    return (x[:half], x[half:]) if axis == 0 else (x[:, :half], x[:, half:])


def spread(ur, ui, axis):
    ar, br = halves(ur, axis)
    ai, bi = halves(ui, axis)
    first = lax.broadcasted_iota(jnp.int32, ar.shape, axis) == 0
    yr = jnp.concatenate(
        [ar + jnp.where(first, 0.0, bi), jnp.where(first, br, ar - bi)], axis=axis
    )
    yi = jnp.concatenate(
        [ai - jnp.where(first, 0.0, br), jnp.where(first, bi, ai + br)], axis=axis
    )
    return yr, yi


def gather_pairs(zr, zi, axis):
    ar, br = halves(zr, axis)
    ai, bi = halves(zi, axis)
    first = lax.broadcasted_iota(jnp.int32, ar.shape, axis) == 0
    xr = jnp.concatenate(
        [ar + jnp.where(first, 0.0, br), jnp.where(first, br, bi - ai)], axis=axis
    )
    xi = jnp.concatenate(
        [ai + jnp.where(first, 0.0, bi), jnp.where(first, bi, ar - br)], axis=axis
    )
    return xr, xi


def sweep_kernel(
    corner_ref, alive_ref, ext_ref, probe_ref, intensity_ref,
    left_ref, right_ref, left_t_ref, right_t_ref, perm_ref, perm_t_ref,
    totals_ref, grad_ref, power_ref,
):
    window = probe_ref.shape[1]
    slots = intensity_ref.shape[0]
    last_top = ext_ref.shape[1] - window - SUBLANES
    last_start = ext_ref.shape[2] - window - LANES
    totals_ref[...] = jnp.zeros_like(totals_ref)
    grad_ref[...] = jnp.zeros_like(grad_ref)
    power_ref[...] = probe_ref[0] * probe_ref[0] + probe_ref[1] * probe_ref[1]
    lane = lax.broadcasted_iota(jnp.int32, (window + SUBLANES, LANES), 1)
    pieces = (window // SUBLANES, SUBLANES, LANES)
    sublane = lax.broadcasted_iota(jnp.int32, pieces, 1)
    sublane_tall = lax.broadcasted_iota(jnp.int32, (pieces[0] + 1, *pieces[1:]), 1)

    def visit(slot, carry):
        @pl.when(alive_ref[slot] != 0)
        def _():
            row = corner_ref[slot, 0]
            column = corner_ref[slot, 1]
            top = jnp.minimum((row // SUBLANES) * SUBLANES, last_top)
            down = row - top
            top = pl.multiple_of(top, SUBLANES)
            start = jnp.minimum((column // LANES) * LANES, last_start)
            shift = column - start
            start = pl.multiple_of(start, LANES)
            weight = alive_ref[slot].astype(jnp.float32)
            count = window // LANES
            tall = window + SUBLANES
            groups = window // SUBLANES

            def strip(plane, j):
                return (plane, pl.ds(top, tall), pl.ds(start + j * LANES, LANES))

            def fetch(plane):
                blocks = [
                    pltpu.roll(ext_ref[strip(plane, j)], lax.rem(LANES - shift, LANES), 1)
                    for j in range(count + 1)
                ]
                out = []
                for j in range(count):
                    block = jnp.where(lane < LANES - shift, blocks[j], blocks[j + 1])
                    block = block.reshape(groups + 1, SUBLANES, LANES)
                    block = pltpu.roll(block, lax.rem(SUBLANES - down, SUBLANES), 1)
                    block = jnp.where(sublane < SUBLANES - down, block[:-1], block[1:])
                    out.append(block.reshape(window, LANES))
                return jnp.concatenate(out, axis=1)

            def deposit(plane, value):
                blocks = []
                none = jnp.zeros((1, SUBLANES, LANES), jnp.float32)
                for j in range(count):
                    block = value[:, j * LANES : (j + 1) * LANES]
                    block = block.reshape(groups, SUBLANES, LANES)
                    block = pltpu.roll(block, lax.rem(down, SUBLANES), 1)
                    here = jnp.concatenate([block, none], axis=0)
                    before = jnp.concatenate([none, block], axis=0)
                    block = jnp.where(sublane_tall >= down, here, before)
                    blocks.append(pltpu.roll(block.reshape(tall, LANES), lax.rem(shift, LANES), 1))
                for j in range(count + 1):
                    here = blocks[j] if j < count else jnp.zeros_like(blocks[0])
                    before = blocks[j - 1] if j > 0 else jnp.zeros_like(blocks[0])
                    totals_ref[strip(plane, j)] += jnp.where(lane >= shift, here, before)

            patch_r, patch_i = fetch(0), fetch(1)
            probe_r, probe_i = probe_ref[0], probe_ref[1]
            exit_r = probe_r * patch_r - probe_i * patch_i
            exit_i = probe_r * patch_i + probe_i * patch_r
            yr, yi = spread(
                times_left(left_ref[...], exit_r), times_left(left_ref[...], exit_i), 0
            )
            zr, zi = spread(
                times_right(yr, right_ref[...]), times_right(yi, right_ref[...]), 1
            )
            amplitude = jnp.sqrt(intensity_ref[slot])
            hi, mid = split(amplitude)
            rest = amplitude - hi.astype(jnp.float32) - mid.astype(jnp.float32)
            low = rest.astype(jnp.bfloat16)
            rows = [dot(perm_ref[...], part).astype(jnp.bfloat16) for part in (hi, mid, low)]
            amplitude = sum(dot(part, perm_t_ref[...]) for part in rows)
            magnitude = jnp.sqrt(zr * zr + zi * zi)
            factor = amplitude / jnp.maximum(magnitude, FLOOR)
            zr, zi = gather_pairs(zr * factor, zi * factor, 0)
            yr, yi = times_left(left_t_ref[...], zr), times_left(left_t_ref[...], zi)
            yr, yi = gather_pairs(yr, yi, 1)
            back_r, back_i = times_right(yr, right_t_ref[...]), times_right(yi, right_t_ref[...])
            diff_r = weight * (back_r - exit_r)
            diff_i = weight * (back_i - exit_i)
            deposit(0, probe_r * diff_r + probe_i * diff_i)
            deposit(1, probe_r * diff_i - probe_i * diff_r)
            deposit(2, weight * power_ref[...])
            grad_ref[0] += patch_r * diff_r + patch_i * diff_i
            grad_ref[1] += patch_r * diff_i - patch_i * diff_r
            grad_ref[2] += weight * (patch_r * patch_r + patch_i * patch_i)

        return carry

    lax.fori_loop(0, slots, visit, 0)


def sweep(corners, occupied, extended, probe_field, intensity):
    window = probe_field.shape[1]
    rows, columns = extended.shape[1:]
    smem = pl.BlockSpec(memory_space=pltpu.SMEM)
    vmem = pl.BlockSpec(memory_space=pltpu.VMEM)
    consts = [jnp.asarray(t) for t in tables(window)]
    return pl.pallas_call(
        sweep_kernel,
        out_shape=(
            jax.ShapeDtypeStruct((3, rows, columns), jnp.float32),
            jax.ShapeDtypeStruct((3, window, window), jnp.float32),
        ),
        in_specs=[smem, smem] + [vmem] * (3 + len(consts)),
        out_specs=(vmem, vmem),
        scratch_shapes=[pltpu.VMEM((window, window), jnp.float32)],
        compiler_params=pltpu.CompilerParams(vmem_limit_bytes=48 * 1024 * 1024),
        name="sweep",
    )(corners, occupied, extended, probe_field, intensity, *consts)


class Shift:
    def __init__(self, net, src, dst, axis, delta, also=None):
        self.net, self.src, self.dst = net, src, dst
        self.slot = net.slot()
        here, count = net.place[axis], net.size[axis]
        self.sends = here + delta < count if delta > 0 else here > 0
        self.gets = here > 0 if delta > 0 else here - delta < count
        if also is not None:
            self.sends = jnp.logical_and(self.sends, also)
            self.gets = jnp.logical_and(self.gets, also)
        self.target = net.target(axis, here + delta)

    def copy(self):
        return pltpu.make_async_remote_copy(
            src_ref=self.src,
            dst_ref=self.dst,
            send_sem=self.net.send_sem.at[self.slot],
            recv_sem=self.net.recv_sem.at[self.slot],
            device_id=self.target,
            device_id_type=pl.DeviceIdType.MESH,
        )

    def start(self):
        pl.when(self.sends)(lambda: self.copy().start())
        self.net.started.append(self)

    def arrived(self):
        pl.when(self.gets)(lambda: self.copy().wait_recv())

    def sent(self):
        pl.when(self.sends)(lambda: self.copy().wait_send())


class Net:
    def __init__(self, size, send_sem, recv_sem):
        self.size = size
        self.place = {axis: lax.axis_index(axis) for axis in size}
        self.send_sem, self.recv_sem = send_sem, recv_sem
        self.used = 0
        self.started = []

    def slot(self):
        self.used += 1
        return self.used - 1

    def target(self, axis, index):
        return tuple(index if name == axis else self.place[name] for name in self.size)

    def bits(self):
        out = []
        for axis, count in self.size.items():
            bit = 1
            while bit < count:
                value = (self.place[axis] // bit) % 2
                out.append((axis, self.place[axis] + bit * (1 - 2 * value), value))
                bit *= 2
        return out

    def greet(self, partners):
        barrier = pltpu.get_barrier_semaphore()
        expected = jnp.int32(0)
        for axis, count in self.size.items():
            here = self.place[axis]
            for delta, there in ((-1, here > 0), (1, here < count - 1)):
                target = self.target(axis, here + delta)

                @pl.when(there)
                def _(target=target):
                    pl.semaphore_signal(
                        barrier, inc=1, device_id=target, device_id_type=pl.DeviceIdType.MESH
                    )

                expected += there.astype(jnp.int32)
        for axis, other, _ in partners:
            pl.semaphore_signal(
                barrier,
                inc=1,
                device_id=self.target(axis, other),
                device_id_type=pl.DeviceIdType.MESH,
            )
        pl.semaphore_wait(barrier, expected + len(partners))

    def finish(self):
        for shift in self.started:
            shift.sent()


def halo(net, ext_ref, margin, between):
    rows, columns = ext_ref.shape[1] - 2 * margin, ext_ref.shape[2] - 2 * margin
    tall, broad = pl.ds(margin, rows), pl.ds(margin, columns)
    near, far = {}, {}
    for axis_name, extent in (("ty", rows), ("tx", columns)):
        near[axis_name] = {-1: pl.ds(margin, margin), 1: pl.ds(extent, margin)}
        far[axis_name] = {-1: pl.ds(extent + margin, margin), 1: pl.ds(0, margin)}
    side = []
    for delta in (-1, 1):
        src = ext_ref.at[:, tall, near["tx"][delta]]
        side.append(Shift(net, src, ext_ref.at[:, tall, far["tx"][delta]], "tx", delta))
    upright = []
    for delta in (-1, 1):
        src = ext_ref.at[:, near["ty"][delta], broad]
        upright.append(Shift(net, src, ext_ref.at[:, far["ty"][delta], broad], "ty", delta))
    for shift in side + upright:
        shift.start()
    between()
    for shift, lanes in zip(side, (pl.ds(columns + margin, margin), pl.ds(0, margin))):
        shift.arrived()
        for delta in (-1, 1):
            src = ext_ref.at[:, near["ty"][delta], lanes]
            dst = ext_ref.at[:, far["ty"][delta], lanes]
            corner = Shift(net, src, dst, "ty", delta, also=shift.gets)
            corner.start()
            upright.append(corner)
    between()
    for shift in upright:
        shift.arrived()


def first_halo_kernel(size, margin, specimen_ref, ext_ref, send_sem, recv_sem):
    net = Net(size, send_sem, recv_sem)
    rows, columns = specimen_ref.shape[1:]
    ext_ref[:, margin : margin + rows, margin : margin + columns] = specimen_ref[...]
    net.greet([])
    halo(net, ext_ref, margin, lambda: None)
    net.finish()


def reduce_steps(net, partners, grads_ref, acc_ref, whole_ref, inbox_refs):
    low, height = 0, grads_ref.shape[1]
    held = grads_ref
    undo = []
    for step, (axis, other, value) in enumerate(partners):
        half = height // 2
        halving = half % SUBLANES == 0
        kept, sent = low, low
        if halving:
            kept = pl.multiple_of(low + value * half, SUBLANES)
            sent = pl.multiple_of(low + (1 - value) * half, SUBLANES)
            height = half
        slot = net.slot()
        inbox = inbox_refs[step]
        source = held.at[:, pl.ds(sent, height), :]
        if not halving:
            outbox = inbox.at[1]
            outbox[...] = held[:, pl.ds(kept, height), :]
            source, inbox = outbox, inbox.at[0]
        copy = pltpu.make_async_remote_copy(
            src_ref=source,
            dst_ref=inbox,
            send_sem=net.send_sem.at[slot],
            recv_sem=net.recv_sem.at[slot],
            device_id=net.target(axis, other),
            device_id_type=pl.DeviceIdType.MESH,
        )
        copy.start()
        yield
        copy.wait()
        acc_ref[:, pl.ds(kept, height), :] = held[:, pl.ds(kept, height), :] + inbox[...]
        held = acc_ref
        if halving:
            undo.append((axis, other, kept, height, low))
        low = kept
    whole_ref[:, pl.ds(low, height), :] = acc_ref[:, pl.ds(low, height), :]
    for axis, other, kept, height, _ in reversed(undo):
        slot = net.slot()
        part = whole_ref.at[:, pl.ds(kept, height), :]
        copy = pltpu.make_async_remote_copy(
            src_ref=part,
            dst_ref=part,
            send_sem=net.send_sem.at[slot],
            recv_sem=net.recv_sem.at[slot],
            device_id=net.target(axis, other),
            device_id_type=pl.DeviceIdType.MESH,
        )
        copy.start()
        yield
        copy.wait()


def settle_kernel(
    size, margin, last, totals_ref, grads_ref, ext_ref, probe_ref, out_ref, probe_out_ref,
    from_rows_ref, strip_ref, from_columns_ref, acc_ref, whole_ref, *rest,
):
    *inbox_refs, send_sem, recv_sem = rest
    net = Net(size, send_sem, recv_sem)
    partners = net.bits()
    rows, columns = ext_ref.shape[1] - 2 * margin, ext_ref.shape[2] - 2 * margin
    shifts = {}
    up, down = 0, 1
    for where, delta, start in ((down, -1, 0), (up, 1, rows + margin)):
        src = totals_ref.at[:, pl.ds(start, margin), :]
        shifts["rows", where] = Shift(net, src, from_rows_ref.at[where], "ty", delta)
    bands = ((0, margin), (margin, rows - 2 * margin), (rows - margin, margin))
    for band, (first, height) in enumerate(bands):
        for where, delta, start in ((1, -1, 0), (0, 1, columns + margin)):
            lanes = pl.ds(start, margin)
            if band == 1:
                src = totals_ref.at[:, pl.ds(margin + first, height), lanes]
            else:
                src = strip_ref.at[band // 2, :, :, lanes]
            dst = from_columns_ref.at[where, :, pl.ds(first, height), :]
            shifts["columns", band, where] = Shift(net, src, dst, "tx", delta)
    for key, ref, axis in (
        ((up, down), from_rows_ref, "ty"),
        ((0, 1), from_columns_ref, "tx"),
    ):
        for where in key:
            missing = net.place[axis] == (0 if where == 0 else size[axis] - 1)

            @pl.when(missing)
            def _(ref=ref, where=where):
                ref[where] = jnp.zeros(ref.shape[1:], jnp.float32)

    net.greet(partners)
    reducing = reduce_steps(net, partners, grads_ref, acc_ref, whole_ref, inbox_refs)

    def step():
        next(reducing, None)

    for where in (up, down):
        shifts["rows", where].start()
    for where in (0, 1):
        shifts["columns", 1, where].start()
    step()
    shift_out = 0 if last else margin

    def renew(band, side):
        first, height = bands[band]
        left, wide = ((0, margin), (margin, columns - 2 * margin), (columns - margin, margin))[side]
        if band == 1:
            total = totals_ref[:, pl.ds(margin + first, height), pl.ds(margin + left, wide)]
        else:
            total = strip_ref[band // 2, :, :, pl.ds(margin + left, wide)]
        if side != 1:
            total = total + from_columns_ref[side // 2, :, pl.ds(first, height), :]
        old = ext_ref[:, pl.ds(margin + first, height), pl.ds(margin + left, wide)]
        new = old + total[:2] / (total[2:] + SPECIMEN_REG)
        out_ref[:, pl.ds(shift_out + first, height), pl.ds(shift_out + left, wide)] = new

    renew(1, 1)
    step()
    for where, start in ((up, margin), (down, rows)):
        shifts["rows", where].arrived()
        strip_ref[where] = totals_ref[:, pl.ds(start, margin), :] + from_rows_ref[where]
        for side in (0, 1):
            shifts["columns", 2 * where, side].start()
    step()
    renew(0, 1)
    renew(2, 1)
    step()
    for band in (1, 0, 2):
        for side in (0, 1):
            shifts["columns", band, side].arrived()
            renew(band, 2 * side)
        step()
    if not last:
        def between():
            step()
            step()

        halo(net, out_ref, margin, between)
    for _ in reducing:
        pass
    whole = whole_ref[...]
    probe_out_ref[...] = probe_ref[...] + whole[:2] / (whole[2:] + PROBE_REG)
    net.finish()


VMEM = pl.BlockSpec(memory_space=pltpu.VMEM)
ROOM = 48 * 1024 * 1024


def first_halo(size, specimen, margin):
    planes, rows, columns = specimen.shape
    return pl.pallas_call(
        functools.partial(first_halo_kernel, size, margin),
        out_shape=jax.ShapeDtypeStruct(
            (planes, rows + 2 * margin, columns + 2 * margin), jnp.float32
        ),
        in_specs=[VMEM],
        out_specs=VMEM,
        scratch_shapes=[pltpu.SemaphoreType.DMA((8,)), pltpu.SemaphoreType.DMA((8,))],
        compiler_params=pltpu.CompilerParams(
            collective_id=0, has_side_effects=True, vmem_limit_bytes=ROOM
        ),
        name="first_halo",
    )(specimen)


def settle(size, totals, grads, extended, probe_field, margin, last):
    window = probe_field.shape[1]
    wide = extended.shape[2]
    rows, columns = extended.shape[1] - 2 * margin, wide - 2 * margin
    inboxes = []
    height = window
    copies = 16
    for count in size.values():
        for _ in range(int(math.log2(count))):
            if (height // 2) % SUBLANES == 0:
                height //= 2
                inboxes.append(pltpu.VMEM((3, height, window), jnp.float32))
            else:
                inboxes.append(pltpu.VMEM((2, 3, height, window), jnp.float32))
            copies += 2
    out = (2, rows, columns) if last else extended.shape
    return pl.pallas_call(
        functools.partial(settle_kernel, size, margin, last),
        out_shape=(
            jax.ShapeDtypeStruct(out, jnp.float32),
            jax.ShapeDtypeStruct(probe_field.shape, jnp.float32),
        ),
        in_specs=[VMEM] * 4,
        out_specs=(VMEM, VMEM),
        scratch_shapes=[
            pltpu.VMEM((2, 3, margin, wide), jnp.float32),
            pltpu.VMEM((2, 3, margin, wide), jnp.float32),
            pltpu.VMEM((2, 3, rows, margin), jnp.float32),
            pltpu.VMEM(grads.shape, jnp.float32),
            pltpu.VMEM(grads.shape, jnp.float32),
            *inboxes,
            pltpu.SemaphoreType.DMA((copies,)),
            pltpu.SemaphoreType.DMA((copies,)),
        ],
        compiler_params=pltpu.CompilerParams(
            collective_id=2 if last else 1, has_side_effects=True, vmem_limit_bytes=ROOM
        ),
        name="settle_last" if last else "settle",
    )(totals, grads, extended, probe_field)


def body(size, specimen, probe_field, intensity, positions, occupied_slots):
    tile_rows = specimen.shape[1]
    tile_columns = specimen.shape[2]
    window = probe_field.shape[1]
    margin = window // 2
    row_start = lax.axis_index("ty") * tile_rows - margin
    column_start = lax.axis_index("tx") * tile_columns - margin
    corners = positions - jnp.stack([row_start, column_start])[None, :]
    extended = first_halo(size, specimen, margin)
    for iteration in range(ITERS):
        totals, grads = sweep(corners, occupied_slots, extended, probe_field, intensity)
        extended, probe_field = settle(
            size, totals, grads, extended, probe_field, margin, iteration == ITERS - 1
        )
    return (extended, probe_field)


def solution(mesh):
    return jax.shard_map(
        functools.partial(body, dict(mesh.shape)),
        mesh=mesh,
        in_specs=(
            P(None, "ty", "tx"),
            P(),
            P(("ty", "tx"), None, None),
            P(("ty", "tx"), None),
            P(("ty", "tx")),
        ),
        out_specs=(P(None, "ty", "tx"), P()),
        check_vma=False,
    )
```

```python
import functools
import math

import jax
import jax.numpy as jnp
import ml_dtypes
import numpy as np
from jax import lax
from jax.experimental import pallas as pl
from jax.experimental.pallas import tpu as pltpu
from jax.sharding import PartitionSpec as P

ITERS = 2


FLOOR = 0.2
SPECIMEN_REG = 0.5
PROBE_REG = 1.0
LANES = 128
SUBLANES = 8


def split_np(table):
    hi = table.astype(ml_dtypes.bfloat16)
    lo = (table - hi.astype(np.float64)).astype(ml_dtypes.bfloat16)
    return hi, lo


def tables(window):
    half = window // 2
    j = np.arange(half)[:, None]
    m = np.arange(window)[None, :]
    angle = 2.0 * math.pi * ((j * m) % window) / window
    lower = np.sin(angle)
    lower[0] = np.cos(math.pi * m[0])
    real_dft = np.concatenate([np.cos(angle), lower]) / math.sqrt(window)
    hi, lo = split_np(real_dft)
    wide = np.concatenate([hi, hi, lo], axis=1)
    hi_t, lo_t = hi.T.copy(), lo.T.copy()
    wide_t = np.concatenate([hi_t, hi_t, lo_t], axis=1)
    order = np.concatenate([np.arange(half + 1), np.arange(window - 1, half, -1)])
    perm = np.zeros((window, window), ml_dtypes.bfloat16)
    perm[np.arange(window), order] = 1
    return (
        wide,
        wide.T.copy(),
        wide_t,
        wide_t.T.copy(),
        perm,
        perm.T.copy(),
    )


def dot(a, b):
    return jnp.dot(a, b, preferred_element_type=jnp.float32)


def split(x):
    hi = x.astype(jnp.bfloat16)
    return hi, (x - hi.astype(jnp.float32)).astype(jnp.bfloat16)


def times_left(wide, x):
    hi, lo = split(x)
    return dot(wide, jnp.concatenate([hi, lo, hi], axis=0))


def times_right(x, wide):
    hi, lo = split(x)
    return dot(jnp.concatenate([hi, lo, hi], axis=1), wide)


def halves(x, axis):
    half = x.shape[axis] // 2
    return (x[:half], x[half:]) if axis == 0 else (x[:, :half], x[:, half:])


def spread(ur, ui, axis):
    ar, br = halves(ur, axis)
    ai, bi = halves(ui, axis)
    first = lax.broadcasted_iota(jnp.int32, ar.shape, axis) == 0
    yr = jnp.concatenate(
        [ar + jnp.where(first, 0.0, bi), jnp.where(first, br, ar - bi)], axis=axis
    )
    yi = jnp.concatenate(
        [ai - jnp.where(first, 0.0, br), jnp.where(first, bi, ai + br)], axis=axis
    )
    return yr, yi


def gather_pairs(zr, zi, axis):
    ar, br = halves(zr, axis)
    ai, bi = halves(zi, axis)
    first = lax.broadcasted_iota(jnp.int32, ar.shape, axis) == 0
    xr = jnp.concatenate(
        [ar + jnp.where(first, 0.0, br), jnp.where(first, br, bi - ai)], axis=axis
    )
    xi = jnp.concatenate(
        [ai + jnp.where(first, 0.0, bi), jnp.where(first, bi, ar - br)], axis=axis
    )
    return xr, xi


def sweep_kernel(
    corner_ref, alive_ref, ext_ref, probe_ref, amplitude_ref,
    left_ref, right_ref, left_t_ref, right_t_ref,
    totals_ref, grad_ref, power_ref,
):
    window = probe_ref.shape[1]
    slots = amplitude_ref.shape[0]
    last_top = ext_ref.shape[1] - window - SUBLANES
    last_start = ext_ref.shape[2] - window - LANES
    totals_ref[...] = jnp.zeros_like(totals_ref)
    grad_ref[...] = jnp.zeros_like(grad_ref)
    power_ref[...] = probe_ref[0] * probe_ref[0] + probe_ref[1] * probe_ref[1]
    lane = lax.broadcasted_iota(jnp.int32, (window + SUBLANES, LANES), 1)
    pieces = (window // SUBLANES, SUBLANES, LANES)
    sublane = lax.broadcasted_iota(jnp.int32, pieces, 1)
    sublane_tall = lax.broadcasted_iota(jnp.int32, (pieces[0] + 1, *pieces[1:]), 1)

    def visit(slot, carry):
        @pl.when(alive_ref[slot] != 0)
        def _():
            row = corner_ref[slot, 0]
            column = corner_ref[slot, 1]
            top = jnp.minimum((row // SUBLANES) * SUBLANES, last_top)
            down = row - top
            top = pl.multiple_of(top, SUBLANES)
            start = jnp.minimum((column // LANES) * LANES, last_start)
            shift = column - start
            start = pl.multiple_of(start, LANES)
            weight = alive_ref[slot].astype(jnp.float32)
            count = window // LANES
            tall = window + SUBLANES
            groups = window // SUBLANES

            def strip(plane, j):
                return (plane, pl.ds(top, tall), pl.ds(start + j * LANES, LANES))

            def fetch(plane):
                blocks = [
                    pltpu.roll(ext_ref[strip(plane, j)], lax.rem(LANES - shift, LANES), 1)
                    for j in range(count + 1)
                ]
                out = []
                for j in range(count):
                    block = jnp.where(lane < LANES - shift, blocks[j], blocks[j + 1])
                    block = block.reshape(groups + 1, SUBLANES, LANES)
                    block = pltpu.roll(block, lax.rem(SUBLANES - down, SUBLANES), 1)
                    block = jnp.where(sublane < SUBLANES - down, block[:-1], block[1:])
                    out.append(block.reshape(window, LANES))
                return jnp.concatenate(out, axis=1)

            def deposit(plane, value):
                blocks = []
                none = jnp.zeros((1, SUBLANES, LANES), jnp.float32)
                for j in range(count):
                    block = value[:, j * LANES : (j + 1) * LANES]
                    block = block.reshape(groups, SUBLANES, LANES)
                    block = pltpu.roll(block, lax.rem(down, SUBLANES), 1)
                    here = jnp.concatenate([block, none], axis=0)
                    before = jnp.concatenate([none, block], axis=0)
                    block = jnp.where(sublane_tall >= down, here, before)
                    blocks.append(pltpu.roll(block.reshape(tall, LANES), lax.rem(shift, LANES), 1))
                for j in range(count + 1):
                    here = blocks[j] if j < count else jnp.zeros_like(blocks[0])
                    before = blocks[j - 1] if j > 0 else jnp.zeros_like(blocks[0])
                    totals_ref[strip(plane, j)] += jnp.where(lane >= shift, here, before)

            patch_r, patch_i = fetch(0), fetch(1)
            probe_r, probe_i = probe_ref[0], probe_ref[1]
            exit_r = probe_r * patch_r - probe_i * patch_i
            exit_i = probe_r * patch_i + probe_i * patch_r
            yr, yi = spread(
                times_left(left_ref[...], exit_r), times_left(left_ref[...], exit_i), 0
            )
            zr, zi = spread(
                times_right(yr, right_ref[...]), times_right(yi, right_ref[...]), 1
            )
            amplitude = amplitude_ref[slot]
            magnitude = jnp.sqrt(zr * zr + zi * zi)
            factor = amplitude / jnp.maximum(magnitude, FLOOR)
            zr, zi = gather_pairs(zr * factor, zi * factor, 0)
            yr, yi = times_left(left_t_ref[...], zr), times_left(left_t_ref[...], zi)
            yr, yi = gather_pairs(yr, yi, 1)
            back_r, back_i = times_right(yr, right_t_ref[...]), times_right(yi, right_t_ref[...])
            diff_r = weight * (back_r - exit_r)
            diff_i = weight * (back_i - exit_i)
            deposit(0, probe_r * diff_r + probe_i * diff_i)
            deposit(1, probe_r * diff_i - probe_i * diff_r)
            deposit(2, weight * power_ref[...])
            grad_ref[0] += patch_r * diff_r + patch_i * diff_i
            grad_ref[1] += patch_r * diff_i - patch_i * diff_r
            grad_ref[2] += weight * (patch_r * patch_r + patch_i * patch_i)

        return carry

    lax.fori_loop(0, slots, visit, 0)


def sweep(corners, occupied, extended, probe_field, amplitude):
    window = probe_field.shape[1]
    rows, columns = extended.shape[1:]
    smem = pl.BlockSpec(memory_space=pltpu.SMEM)
    vmem = pl.BlockSpec(memory_space=pltpu.VMEM)
    consts = [jnp.asarray(t) for t in tables(window)[:4]]
    return pl.pallas_call(
        sweep_kernel,
        out_shape=(
            jax.ShapeDtypeStruct((3, rows, columns), jnp.float32),
            jax.ShapeDtypeStruct((3, window, window), jnp.float32),
        ),
        in_specs=[smem, smem] + [vmem] * (3 + len(consts)),
        out_specs=(vmem, vmem),
        scratch_shapes=[pltpu.VMEM((window, window), jnp.float32)],
        compiler_params=pltpu.CompilerParams(vmem_limit_bytes=48 * 1024 * 1024),
        name="sweep",
    )(corners, occupied, extended, probe_field, amplitude, *consts)


class Shift:
    def __init__(self, net, src, dst, axis, delta, also=None):
        self.net, self.src, self.dst = net, src, dst
        self.slot = net.slot()
        here, count = net.place[axis], net.size[axis]
        self.sends = here + delta < count if delta > 0 else here > 0
        self.gets = here > 0 if delta > 0 else here - delta < count
        if also is not None:
            self.sends = jnp.logical_and(self.sends, also)
            self.gets = jnp.logical_and(self.gets, also)
        self.target = net.target(axis, here + delta)

    def copy(self):
        return pltpu.make_async_remote_copy(
            src_ref=self.src,
            dst_ref=self.dst,
            send_sem=self.net.send_sem.at[self.slot],
            recv_sem=self.net.recv_sem.at[self.slot],
            device_id=self.target,
            device_id_type=pl.DeviceIdType.MESH,
        )

    def start(self):
        pl.when(self.sends)(lambda: self.copy().start())
        self.net.started.append(self)

    def arrived(self):
        pl.when(self.gets)(lambda: self.copy().wait_recv())

    def sent(self):
        pl.when(self.sends)(lambda: self.copy().wait_send())


class Net:
    def __init__(self, size, send_sem, recv_sem):
        self.size = size
        self.place = {axis: lax.axis_index(axis) for axis in size}
        self.send_sem, self.recv_sem = send_sem, recv_sem
        self.used = 0
        self.started = []

    def slot(self):
        self.used += 1
        return self.used - 1

    def target(self, axis, index):
        return tuple(index if name == axis else self.place[name] for name in self.size)

    def bits(self):
        out = []
        for axis, count in self.size.items():
            bit = 1
            while bit < count:
                value = (self.place[axis] // bit) % 2
                out.append((axis, self.place[axis] + bit * (1 - 2 * value), value))
                bit *= 2
        rows = [entry for entry in out if entry[0] == "ty"]
        columns = [entry for entry in out if entry[0] == "tx"]
        return rows[:1] + rows[:1:-1] + columns + rows[1:2]

    def greet(self, partners):
        barrier = pltpu.get_barrier_semaphore()
        expected = jnp.int32(0)
        for axis, count in self.size.items():
            here = self.place[axis]
            for delta, there in ((-1, here > 0), (1, here < count - 1)):
                target = self.target(axis, here + delta)

                @pl.when(there)
                def _(target=target):
                    pl.semaphore_signal(
                        barrier, inc=1, device_id=target, device_id_type=pl.DeviceIdType.MESH
                    )

                expected += there.astype(jnp.int32)
        for axis, other, _ in partners:
            pl.semaphore_signal(
                barrier,
                inc=1,
                device_id=self.target(axis, other),
                device_id_type=pl.DeviceIdType.MESH,
            )
        pl.semaphore_wait(barrier, expected + len(partners))

    def finish(self):
        for shift in self.started:
            shift.sent()


def halo(net, ext_ref, margin, between):
    rows, columns = ext_ref.shape[1] - 2 * margin, ext_ref.shape[2] - 2 * margin
    tall, broad = pl.ds(margin, rows), pl.ds(margin, columns)
    near, far = {}, {}
    for axis_name, extent in (("ty", rows), ("tx", columns)):
        near[axis_name] = {-1: pl.ds(margin, margin), 1: pl.ds(extent, margin)}
        far[axis_name] = {-1: pl.ds(extent + margin, margin), 1: pl.ds(0, margin)}
    side = []
    for delta in (-1, 1):
        src = ext_ref.at[:, tall, near["tx"][delta]]
        side.append(Shift(net, src, ext_ref.at[:, tall, far["tx"][delta]], "tx", delta))
    upright = []
    for delta in (-1, 1):
        src = ext_ref.at[:, near["ty"][delta], broad]
        upright.append(Shift(net, src, ext_ref.at[:, far["ty"][delta], broad], "ty", delta))
    for shift in side + upright:
        shift.start()
    between()
    for shift, lanes in zip(side, (pl.ds(columns + margin, margin), pl.ds(0, margin))):
        shift.arrived()
        for delta in (-1, 1):
            src = ext_ref.at[:, near["ty"][delta], lanes]
            dst = ext_ref.at[:, far["ty"][delta], lanes]
            corner = Shift(net, src, dst, "ty", delta, also=shift.gets)
            corner.start()
            upright.append(corner)
    between()
    for shift in upright:
        shift.arrived()


def first_halo_kernel(
    size, margin, specimen_ref, intensity_ref, perm_ref, perm_t_ref, ext_ref, amplitude_ref,
    send_sem, recv_sem,
):
    net = Net(size, send_sem, recv_sem)
    rows, columns = specimen_ref.shape[1:]
    ext_ref[:, margin : margin + rows, margin : margin + columns] = specimen_ref[...]
    net.greet([])

    def order(first, last):
        def visit(slot, carry):
            amplitude = jnp.sqrt(intensity_ref[slot])
            hi, mid = split(amplitude)
            rest = amplitude - hi.astype(jnp.float32) - mid.astype(jnp.float32)
            low = rest.astype(jnp.bfloat16)
            rows = [dot(perm_ref[...], part).astype(jnp.bfloat16) for part in (hi, mid, low)]
            amplitude_ref[slot] = sum(dot(part, perm_t_ref[...]) for part in rows)
            return carry

        lax.fori_loop(first, last, visit, 0)

    slots = intensity_ref.shape[0]
    parts = iter([(0, slots - 2), (slots - 2, slots)])
    halo(net, ext_ref, margin, lambda: order(*next(parts)))
    net.finish()


def reduce_steps(net, partners, grads_ref, acc_ref, whole_ref, inbox_refs):
    low, height = 0, grads_ref.shape[1]
    held = grads_ref
    undo = []
    for step, (axis, other, value) in enumerate(partners):
        half = height // 2
        halving = half % SUBLANES == 0
        kept, sent = low, low
        if halving:
            kept = pl.multiple_of(low + value * half, SUBLANES)
            sent = pl.multiple_of(low + (1 - value) * half, SUBLANES)
            height = half
        slot = net.slot()
        inbox = inbox_refs[step]
        source = held.at[:, pl.ds(sent, height), :]
        if not halving:
            outbox = inbox.at[1]
            outbox[...] = held[:, pl.ds(kept, height), :]
            source, inbox = outbox, inbox.at[0]
        copy = pltpu.make_async_remote_copy(
            src_ref=source,
            dst_ref=inbox,
            send_sem=net.send_sem.at[slot],
            recv_sem=net.recv_sem.at[slot],
            device_id=net.target(axis, other),
            device_id_type=pl.DeviceIdType.MESH,
        )
        copy.start()
        yield
        copy.wait()
        acc_ref[:, pl.ds(kept, height), :] = held[:, pl.ds(kept, height), :] + inbox[...]
        held = acc_ref
        if halving:
            undo.append((axis, other, kept, height, low))
        low = kept
    whole_ref[:, pl.ds(low, height), :] = acc_ref[:, pl.ds(low, height), :]
    for axis, other, kept, height, _ in reversed(undo):
        slot = net.slot()
        part = whole_ref.at[:, pl.ds(kept, height), :]
        copy = pltpu.make_async_remote_copy(
            src_ref=part,
            dst_ref=part,
            send_sem=net.send_sem.at[slot],
            recv_sem=net.recv_sem.at[slot],
            device_id=net.target(axis, other),
            device_id_type=pl.DeviceIdType.MESH,
        )
        copy.start()
        yield
        copy.wait()


def settle_kernel(
    size, margin, last, totals_ref, grads_ref, ext_ref, probe_ref, out_ref, probe_out_ref,
    from_rows_ref, strip_ref, from_columns_ref, acc_ref, whole_ref, *rest,
):
    *inbox_refs, send_sem, recv_sem = rest
    net = Net(size, send_sem, recv_sem)
    partners = net.bits()
    rows, columns = ext_ref.shape[1] - 2 * margin, ext_ref.shape[2] - 2 * margin
    shifts = {}
    up, down = 0, 1
    pieces = (pl.ds(0, margin), pl.ds(columns + margin, margin), pl.ds(margin, columns))
    for where, delta, start in ((down, -1, 0), (up, 1, rows + margin)):
        for piece, lanes in enumerate(pieces):
            src = totals_ref.at[:, pl.ds(start, margin), lanes]
            dst = from_rows_ref.at[where, :, :, lanes]
            shifts["rows", where, piece] = Shift(net, src, dst, "ty", delta)
    bands = ((0, margin), (margin, rows - 2 * margin), (rows - margin, margin))
    for band, (first, height) in enumerate(bands):
        for where, delta, start in ((1, -1, 0), (0, 1, columns + margin)):
            lanes = pl.ds(start, margin)
            if band == 1:
                src = totals_ref.at[:, pl.ds(margin + first, height), lanes]
            else:
                src = strip_ref.at[band // 2, :, :, lanes]
            dst = from_columns_ref.at[where, :, pl.ds(first, height), :]
            shifts["columns", band, where] = Shift(net, src, dst, "tx", delta)
    for key, ref, axis in (
        ((up, down), from_rows_ref, "ty"),
        ((0, 1), from_columns_ref, "tx"),
    ):
        for where in key:
            missing = net.place[axis] == (0 if where == 0 else size[axis] - 1)

            @pl.when(missing)
            def _(ref=ref, where=where):
                ref[where] = jnp.zeros(ref.shape[1:], jnp.float32)

    net.greet(partners)
    reducing = reduce_steps(net, partners, grads_ref, acc_ref, whole_ref, inbox_refs)

    def step():
        next(reducing, None)

    for piece in (0, 1):
        for where in (up, down):
            shifts["rows", where, piece].start()
    step()
    for where in (0, 1):
        shifts["columns", 1, where].start()
    for where in (up, down):
        shifts["rows", where, 2].start()
    shift_out = 0 if last else margin

    def renew(band, side):
        first, height = bands[band]
        left, wide = ((0, margin), (margin, columns - 2 * margin), (columns - margin, margin))[side]
        if band == 1:
            total = totals_ref[:, pl.ds(margin + first, height), pl.ds(margin + left, wide)]
        else:
            total = strip_ref[band // 2, :, :, pl.ds(margin + left, wide)]
        if side != 1:
            total = total + from_columns_ref[side // 2, :, pl.ds(first, height), :]
        old = ext_ref[:, pl.ds(margin + first, height), pl.ds(margin + left, wide)]
        new = old + total[:2] / (total[2:] + SPECIMEN_REG)
        out_ref[:, pl.ds(shift_out + first, height), pl.ds(shift_out + left, wide)] = new

    def join(where, piece):
        lanes = pieces[piece]
        start = margin if where == up else rows
        shifts["rows", where, piece].arrived()
        strip_ref[where, :, :, lanes] = (
            totals_ref[:, pl.ds(start, margin), lanes] + from_rows_ref[where, :, :, lanes]
        )

    step()
    renew(1, 1)
    step()
    for side in (0, 1):
        for where in (up, down):
            join(where, side)
            shifts["columns", 2 * where, 1 - side].start()
    step()
    step()
    for where in (up, down):
        join(where, 2)
        renew(2 * where, 1)
        step()
    for band in (1, 0, 2):
        for side in (0, 1):
            shifts["columns", band, side].arrived()
            renew(band, 2 * side)
        step()
    if not last:
        def between():
            step()
            step()

        halo(net, out_ref, margin, between)
    for _ in reducing:
        pass
    whole = whole_ref[...]
    probe_out_ref[...] = probe_ref[...] + whole[:2] / (whole[2:] + PROBE_REG)
    net.finish()


VMEM = pl.BlockSpec(memory_space=pltpu.VMEM)
ROOM = 48 * 1024 * 1024


def first_halo(size, specimen, intensity, margin):
    planes, rows, columns = specimen.shape
    return pl.pallas_call(
        functools.partial(first_halo_kernel, size, margin),
        out_shape=(
            jax.ShapeDtypeStruct((planes, rows + 2 * margin, columns + 2 * margin), jnp.float32),
            jax.ShapeDtypeStruct(intensity.shape, jnp.float32),
        ),
        in_specs=[VMEM] * 4,
        out_specs=(VMEM, VMEM),
        scratch_shapes=[pltpu.SemaphoreType.DMA((8,)), pltpu.SemaphoreType.DMA((8,))],
        compiler_params=pltpu.CompilerParams(
            collective_id=0, has_side_effects=True, vmem_limit_bytes=ROOM
        ),
        name="first_halo",
    )(specimen, intensity, *[jnp.asarray(t) for t in tables(intensity.shape[1])[4:]])


def settle(size, totals, grads, extended, probe_field, margin, last):
    window = probe_field.shape[1]
    wide = extended.shape[2]
    rows, columns = extended.shape[1] - 2 * margin, wide - 2 * margin
    inboxes = []
    height = window
    copies = 20
    for count in size.values():
        for _ in range(int(math.log2(count))):
            if (height // 2) % SUBLANES == 0:
                height //= 2
                inboxes.append(pltpu.VMEM((3, height, window), jnp.float32))
            else:
                inboxes.append(pltpu.VMEM((2, 3, height, window), jnp.float32))
            copies += 2
    out = (2, rows, columns) if last else extended.shape
    return pl.pallas_call(
        functools.partial(settle_kernel, size, margin, last),
        out_shape=(
            jax.ShapeDtypeStruct(out, jnp.float32),
            jax.ShapeDtypeStruct(probe_field.shape, jnp.float32),
        ),
        in_specs=[VMEM] * 4,
        out_specs=(VMEM, VMEM),
        scratch_shapes=[
            pltpu.VMEM((2, 3, margin, wide), jnp.float32),
            pltpu.VMEM((2, 3, margin, wide), jnp.float32),
            pltpu.VMEM((2, 3, rows, margin), jnp.float32),
            pltpu.VMEM(grads.shape, jnp.float32),
            pltpu.VMEM(grads.shape, jnp.float32),
            *inboxes,
            pltpu.SemaphoreType.DMA((copies,)),
            pltpu.SemaphoreType.DMA((copies,)),
        ],
        compiler_params=pltpu.CompilerParams(
            collective_id=2 if last else 1, has_side_effects=True, vmem_limit_bytes=ROOM
        ),
        name="settle_last" if last else "settle",
    )(totals, grads, extended, probe_field)


def body(size, specimen, probe_field, intensity, positions, occupied_slots):
    tile_rows = specimen.shape[1]
    tile_columns = specimen.shape[2]
    window = probe_field.shape[1]
    margin = window // 2
    row_start = lax.axis_index("ty") * tile_rows - margin
    column_start = lax.axis_index("tx") * tile_columns - margin
    corners = positions - jnp.stack([row_start, column_start])[None, :]
    extended, amplitude = first_halo(size, specimen, intensity, margin)
    for iteration in range(ITERS):
        totals, grads = sweep(corners, occupied_slots, extended, probe_field, amplitude)
        extended, probe_field = settle(
            size, totals, grads, extended, probe_field, margin, iteration == ITERS - 1
        )
    return (extended, probe_field)


def solution(mesh):
    return jax.shard_map(
        functools.partial(body, dict(mesh.shape)),
        mesh=mesh,
        in_specs=(
            P(None, "ty", "tx"),
            P(),
            P(("ty", "tx"), None, None),
            P(("ty", "tx"), None),
            P(("ty", "tx")),
        ),
        out_specs=(P(None, "ty", "tx"), P()),
        check_vma=False,
    )
```

```python
import functools
import math

import jax
import jax.numpy as jnp
import ml_dtypes
import numpy as np
from jax import lax
from jax.experimental import pallas as pl
from jax.experimental.pallas import tpu as pltpu
from jax.sharding import PartitionSpec as P

ITERS = 2


FLOOR = 0.2
SPECIMEN_REG = 0.5
PROBE_REG = 1.0
LANES = 128
SUBLANES = 8


def split_np(table):
    hi = table.astype(ml_dtypes.bfloat16)
    lo = (table - hi.astype(np.float64)).astype(ml_dtypes.bfloat16)
    return hi, lo


def tables(window):
    half = window // 2
    j = np.arange(half)[:, None]
    m = np.arange(window)[None, :]
    angle = 2.0 * math.pi * ((j * m) % window) / window
    lower = np.sin(angle)
    lower[0] = np.cos(math.pi * m[0])
    real_dft = np.concatenate([np.cos(angle), lower]) / math.sqrt(window)
    hi, lo = split_np(real_dft)
    wide = np.concatenate([hi, hi, lo], axis=1)
    hi_t, lo_t = hi.T.copy(), lo.T.copy()
    wide_t = np.concatenate([hi_t, hi_t, lo_t], axis=1)
    order = np.concatenate([np.arange(half + 1), np.arange(window - 1, half, -1)])
    perm = np.zeros((window, window), ml_dtypes.bfloat16)
    perm[np.arange(window), order] = 1
    return (
        wide,
        wide.T.copy(),
        wide_t,
        wide_t.T.copy(),
        perm,
        perm.T.copy(),
    )


def dot(a, b):
    return jnp.dot(a, b, preferred_element_type=jnp.float32)


def split(x):
    hi = x.astype(jnp.bfloat16)
    return hi, (x - hi.astype(jnp.float32)).astype(jnp.bfloat16)


def times_left(wide, x):
    hi, lo = split(x)
    return dot(wide, jnp.concatenate([hi, lo, hi], axis=0))


def times_right(x, wide):
    hi, lo = split(x)
    return dot(jnp.concatenate([hi, lo, hi], axis=1), wide)


def halves(x, axis):
    half = x.shape[axis] // 2
    return (x[:half], x[half:]) if axis == 0 else (x[:, :half], x[:, half:])


def spread(ur, ui, axis):
    ar, br = halves(ur, axis)
    ai, bi = halves(ui, axis)
    first = lax.broadcasted_iota(jnp.int32, ar.shape, axis) == 0
    yr = jnp.concatenate(
        [ar + jnp.where(first, 0.0, bi), jnp.where(first, br, ar - bi)], axis=axis
    )
    yi = jnp.concatenate(
        [ai - jnp.where(first, 0.0, br), jnp.where(first, bi, ai + br)], axis=axis
    )
    return yr, yi


def gather_pairs(zr, zi, axis):
    ar, br = halves(zr, axis)
    ai, bi = halves(zi, axis)
    first = lax.broadcasted_iota(jnp.int32, ar.shape, axis) == 0
    xr = jnp.concatenate(
        [ar + jnp.where(first, 0.0, br), jnp.where(first, br, bi - ai)], axis=axis
    )
    xi = jnp.concatenate(
        [ai + jnp.where(first, 0.0, bi), jnp.where(first, bi, ar - br)], axis=axis
    )
    return xr, xi


def sweep_kernel(
    corner_ref, alive_ref, ext_ref, probe_ref, amplitude_ref,
    left_ref, right_ref, left_t_ref, right_t_ref,
    totals_ref, grad_ref, power_ref,
):
    window = probe_ref.shape[1]
    slots = amplitude_ref.shape[0]
    last_top = ext_ref.shape[1] - window - SUBLANES
    last_start = ext_ref.shape[2] - window - LANES
    totals_ref[...] = jnp.zeros_like(totals_ref)
    grad_ref[...] = jnp.zeros_like(grad_ref)
    power_ref[...] = probe_ref[0] * probe_ref[0] + probe_ref[1] * probe_ref[1]
    lane = lax.broadcasted_iota(jnp.int32, (window + SUBLANES, LANES), 1)
    pieces = (window // SUBLANES, SUBLANES, LANES)
    sublane = lax.broadcasted_iota(jnp.int32, pieces, 1)
    sublane_tall = lax.broadcasted_iota(jnp.int32, (pieces[0] + 1, *pieces[1:]), 1)

    def visit(slot, carry):
        @pl.when(alive_ref[slot] != 0)
        def _():
            row = corner_ref[slot, 0]
            column = corner_ref[slot, 1]
            top = jnp.minimum((row // SUBLANES) * SUBLANES, last_top)
            down = row - top
            top = pl.multiple_of(top, SUBLANES)
            start = jnp.minimum((column // LANES) * LANES, last_start)
            shift = column - start
            start = pl.multiple_of(start, LANES)
            weight = alive_ref[slot].astype(jnp.float32)
            count = window // LANES
            tall = window + SUBLANES
            groups = window // SUBLANES

            def strip(plane, j):
                return (plane, pl.ds(top, tall), pl.ds(start + j * LANES, LANES))

            def fetch(plane):
                blocks = [
                    pltpu.roll(ext_ref[strip(plane, j)], lax.rem(LANES - shift, LANES), 1)
                    for j in range(count + 1)
                ]
                out = []
                for j in range(count):
                    block = jnp.where(lane < LANES - shift, blocks[j], blocks[j + 1])
                    block = block.reshape(groups + 1, SUBLANES, LANES)
                    block = pltpu.roll(block, lax.rem(SUBLANES - down, SUBLANES), 1)
                    block = jnp.where(sublane < SUBLANES - down, block[:-1], block[1:])
                    out.append(block.reshape(window, LANES))
                return jnp.concatenate(out, axis=1)

            def deposit(plane, value):
                blocks = []
                none = jnp.zeros((1, SUBLANES, LANES), jnp.float32)
                for j in range(count):
                    block = value[:, j * LANES : (j + 1) * LANES]
                    block = block.reshape(groups, SUBLANES, LANES)
                    block = pltpu.roll(block, lax.rem(down, SUBLANES), 1)
                    here = jnp.concatenate([block, none], axis=0)
                    before = jnp.concatenate([none, block], axis=0)
                    block = jnp.where(sublane_tall >= down, here, before)
                    blocks.append(pltpu.roll(block.reshape(tall, LANES), lax.rem(shift, LANES), 1))
                for j in range(count + 1):
                    here = blocks[j] if j < count else jnp.zeros_like(blocks[0])
                    before = blocks[j - 1] if j > 0 else jnp.zeros_like(blocks[0])
                    totals_ref[strip(plane, j)] += jnp.where(lane >= shift, here, before)

            patch_r, patch_i = fetch(0), fetch(1)
            probe_r, probe_i = probe_ref[0], probe_ref[1]
            exit_r = probe_r * patch_r - probe_i * patch_i
            exit_i = probe_r * patch_i + probe_i * patch_r
            yr, yi = spread(
                times_left(left_ref[...], exit_r), times_left(left_ref[...], exit_i), 0
            )
            zr, zi = spread(
                times_right(yr, right_ref[...]), times_right(yi, right_ref[...]), 1
            )
            amplitude = amplitude_ref[slot]
            magnitude = jnp.sqrt(zr * zr + zi * zi)
            factor = amplitude / jnp.maximum(magnitude, FLOOR)
            zr, zi = gather_pairs(zr * factor, zi * factor, 0)
            yr, yi = times_left(left_t_ref[...], zr), times_left(left_t_ref[...], zi)
            yr, yi = gather_pairs(yr, yi, 1)
            back_r, back_i = times_right(yr, right_t_ref[...]), times_right(yi, right_t_ref[...])
            diff_r = weight * (back_r - exit_r)
            diff_i = weight * (back_i - exit_i)
            deposit(0, probe_r * diff_r + probe_i * diff_i)
            deposit(1, probe_r * diff_i - probe_i * diff_r)
            deposit(2, weight * power_ref[...])
            grad_ref[0] += patch_r * diff_r + patch_i * diff_i
            grad_ref[1] += patch_r * diff_i - patch_i * diff_r
            grad_ref[2] += weight * (patch_r * patch_r + patch_i * patch_i)

        return carry

    lax.fori_loop(0, slots, visit, 0)


def sweep(corners, occupied, extended, probe_field, amplitude):
    window = probe_field.shape[1]
    rows, columns = extended.shape[1:]
    smem = pl.BlockSpec(memory_space=pltpu.SMEM)
    vmem = pl.BlockSpec(memory_space=pltpu.VMEM)
    consts = [jnp.asarray(t) for t in tables(window)[:4]]
    return pl.pallas_call(
        sweep_kernel,
        out_shape=(
            jax.ShapeDtypeStruct((3, rows, columns), jnp.float32),
            jax.ShapeDtypeStruct((3, window, window), jnp.float32),
        ),
        in_specs=[smem, smem] + [vmem] * (3 + len(consts)),
        out_specs=(vmem, vmem),
        scratch_shapes=[pltpu.VMEM((window, window), jnp.float32)],
        compiler_params=pltpu.CompilerParams(vmem_limit_bytes=32 * 1024 * 1024),
        name="sweep",
    )(corners, occupied, extended, probe_field, amplitude, *consts)


class Shift:
    def __init__(self, net, src, dst, axis, delta, also=None):
        self.net, self.src, self.dst = net, src, dst
        self.slot = net.slot()
        here, count = net.place[axis], net.size[axis]
        self.sends = here + delta < count if delta > 0 else here > 0
        self.gets = here > 0 if delta > 0 else here - delta < count
        if also is not None:
            self.sends = jnp.logical_and(self.sends, also)
            self.gets = jnp.logical_and(self.gets, also)
        self.target = net.target(axis, here + delta)

    def copy(self):
        return pltpu.make_async_remote_copy(
            src_ref=self.src,
            dst_ref=self.dst,
            send_sem=self.net.send_sem.at[self.slot],
            recv_sem=self.net.recv_sem.at[self.slot],
            device_id=self.target,
            device_id_type=pl.DeviceIdType.MESH,
        )

    def start(self):
        pl.when(self.sends)(lambda: self.copy().start())
        self.net.started.append(self)

    def arrived(self):
        pl.when(self.gets)(lambda: self.copy().wait_recv())

    def sent(self):
        pl.when(self.sends)(lambda: self.copy().wait_send())


class Net:
    def __init__(self, size, send_sem, recv_sem):
        self.size = size
        self.place = {axis: lax.axis_index(axis) for axis in size}
        self.send_sem, self.recv_sem = send_sem, recv_sem
        self.used = 0
        self.started = []

    def slot(self):
        self.used += 1
        return self.used - 1

    def target(self, axis, index):
        return tuple(index if name == axis else self.place[name] for name in self.size)

    def bits(self):
        out = []
        for axis, count in self.size.items():
            bit = 1
            while bit < count:
                value = (self.place[axis] // bit) % 2
                out.append((axis, self.place[axis] + bit * (1 - 2 * value), value))
                bit *= 2
        rows = [entry for entry in out if entry[0] == "ty"]
        columns = [entry for entry in out if entry[0] == "tx"]
        return rows[:1] + rows[:1:-1] + columns + rows[1:2]

    def greet(self, partners):
        barrier = pltpu.get_barrier_semaphore()
        expected = jnp.int32(0)
        for axis, count in self.size.items():
            here = self.place[axis]
            for delta, there in ((-1, here > 0), (1, here < count - 1)):
                target = self.target(axis, here + delta)

                @pl.when(there)
                def _(target=target):
                    pl.semaphore_signal(
                        barrier, inc=1, device_id=target, device_id_type=pl.DeviceIdType.MESH
                    )

                expected += there.astype(jnp.int32)
        for axis, other, _ in partners:
            pl.semaphore_signal(
                barrier,
                inc=1,
                device_id=self.target(axis, other),
                device_id_type=pl.DeviceIdType.MESH,
            )
        pl.semaphore_wait(barrier, expected + len(partners))

    def finish(self):
        for shift in self.started:
            shift.sent()


def halo(net, ext_ref, margin, between):
    rows, columns = ext_ref.shape[1] - 2 * margin, ext_ref.shape[2] - 2 * margin
    tall, broad = pl.ds(margin, rows), pl.ds(margin, columns)
    near, far = {}, {}
    for axis_name, extent in (("ty", rows), ("tx", columns)):
        near[axis_name] = {-1: pl.ds(margin, margin), 1: pl.ds(extent, margin)}
        far[axis_name] = {-1: pl.ds(extent + margin, margin), 1: pl.ds(0, margin)}
    side = []
    for delta in (-1, 1):
        src = ext_ref.at[:, tall, near["tx"][delta]]
        side.append(Shift(net, src, ext_ref.at[:, tall, far["tx"][delta]], "tx", delta))
    upright = []
    for delta in (-1, 1):
        src = ext_ref.at[:, near["ty"][delta], broad]
        upright.append(Shift(net, src, ext_ref.at[:, far["ty"][delta], broad], "ty", delta))
    for shift in side + upright:
        shift.start()
    between()
    for shift, lanes in zip(side, (pl.ds(columns + margin, margin), pl.ds(0, margin))):
        shift.arrived()
        for delta in (-1, 1):
            src = ext_ref.at[:, near["ty"][delta], lanes]
            dst = ext_ref.at[:, far["ty"][delta], lanes]
            corner = Shift(net, src, dst, "ty", delta, also=shift.gets)
            corner.start()
            upright.append(corner)
    between()
    for shift in upright:
        shift.arrived()


def first_halo_kernel(
    size, margin, specimen_ref, intensity_ref, perm_ref, perm_t_ref, ext_ref, amplitude_ref,
    send_sem, recv_sem,
):
    net = Net(size, send_sem, recv_sem)
    rows, columns = specimen_ref.shape[1:]
    ext_ref[:, margin : margin + rows, margin : margin + columns] = specimen_ref[...]
    net.greet([])

    def order(first, last):
        def visit(slot, carry):
            amplitude = jnp.sqrt(intensity_ref[slot])
            hi, mid = split(amplitude)
            rest = amplitude - hi.astype(jnp.float32) - mid.astype(jnp.float32)
            low = rest.astype(jnp.bfloat16)
            rows = [dot(perm_ref[...], part).astype(jnp.bfloat16) for part in (hi, mid, low)]
            amplitude_ref[slot] = sum(dot(part, perm_t_ref[...]) for part in rows)
            return carry

        lax.fori_loop(first, last, visit, 0)

    slots = intensity_ref.shape[0]
    parts = iter([(0, slots - 2), (slots - 2, slots)])
    halo(net, ext_ref, margin, lambda: order(*next(parts)))
    net.finish()


def reduce_steps(net, partners, grads_ref, acc_ref, whole_ref, inbox_refs):
    low, height = 0, grads_ref.shape[1]
    held = grads_ref
    undo = []
    for step, (axis, other, value) in enumerate(partners):
        half = height // 2
        halving = half % SUBLANES == 0
        kept, sent = low, low
        if halving:
            kept = pl.multiple_of(low + value * half, SUBLANES)
            sent = pl.multiple_of(low + (1 - value) * half, SUBLANES)
            height = half
        slot = net.slot()
        inbox = inbox_refs[step]
        source = held.at[:, pl.ds(sent, height), :]
        if not halving:
            outbox = inbox.at[1]
            outbox[...] = held[:, pl.ds(kept, height), :]
            source, inbox = outbox, inbox.at[0]
        copy = pltpu.make_async_remote_copy(
            src_ref=source,
            dst_ref=inbox,
            send_sem=net.send_sem.at[slot],
            recv_sem=net.recv_sem.at[slot],
            device_id=net.target(axis, other),
            device_id_type=pl.DeviceIdType.MESH,
        )
        copy.start()
        yield
        copy.wait()
        acc_ref[:, pl.ds(kept, height), :] = held[:, pl.ds(kept, height), :] + inbox[...]
        held = acc_ref
        if halving:
            undo.append((axis, other, kept, height, low))
        low = kept
    whole_ref[:, pl.ds(low, height), :] = acc_ref[:, pl.ds(low, height), :]
    for axis, other, kept, height, _ in reversed(undo):
        slot = net.slot()
        part = whole_ref.at[:, pl.ds(kept, height), :]
        copy = pltpu.make_async_remote_copy(
            src_ref=part,
            dst_ref=part,
            send_sem=net.send_sem.at[slot],
            recv_sem=net.recv_sem.at[slot],
            device_id=net.target(axis, other),
            device_id_type=pl.DeviceIdType.MESH,
        )
        copy.start()
        yield
        copy.wait()


def settle_kernel(
    size, margin, last, totals_ref, grads_ref, ext_ref, probe_ref, out_ref, probe_out_ref,
    from_rows_ref, strip_ref, from_columns_ref, acc_ref, whole_ref, *rest,
):
    *inbox_refs, send_sem, recv_sem = rest
    net = Net(size, send_sem, recv_sem)
    partners = net.bits()
    rows, columns = ext_ref.shape[1] - 2 * margin, ext_ref.shape[2] - 2 * margin
    shifts = {}
    up, down = 0, 1
    pieces = (pl.ds(0, margin), pl.ds(columns + margin, margin), pl.ds(margin, columns))
    for where, delta, start in ((down, -1, 0), (up, 1, rows + margin)):
        for piece, lanes in enumerate(pieces):
            src = totals_ref.at[:, pl.ds(start, margin), lanes]
            dst = from_rows_ref.at[where, :, :, lanes]
            shifts["rows", where, piece] = Shift(net, src, dst, "ty", delta)
    bands = ((0, margin), (margin, rows - 2 * margin), (rows - margin, margin))
    for band, (first, height) in enumerate(bands):
        for where, delta, start in ((1, -1, 0), (0, 1, columns + margin)):
            lanes = pl.ds(start, margin)
            if band == 1:
                src = totals_ref.at[:, pl.ds(margin + first, height), lanes]
            else:
                src = strip_ref.at[band // 2, :, :, lanes]
            dst = from_columns_ref.at[where, :, pl.ds(first, height), :]
            shifts["columns", band, where] = Shift(net, src, dst, "tx", delta)
    for key, ref, axis in (
        ((up, down), from_rows_ref, "ty"),
        ((0, 1), from_columns_ref, "tx"),
    ):
        for where in key:
            missing = net.place[axis] == (0 if where == 0 else size[axis] - 1)

            @pl.when(missing)
            def _(ref=ref, where=where):
                ref[where] = jnp.zeros(ref.shape[1:], jnp.float32)

    net.greet(partners)
    reducing = reduce_steps(net, partners, grads_ref, acc_ref, whole_ref, inbox_refs)

    def step():
        next(reducing, None)

    for piece in (0, 1):
        for where in (up, down):
            shifts["rows", where, piece].start()
    step()
    for where in (0, 1):
        shifts["columns", 1, where].start()
    for where in (up, down):
        shifts["rows", where, 2].start()
    shift_out = 0 if last else margin

    def renew(band, side):
        first, height = bands[band]
        left, wide = ((0, margin), (margin, columns - 2 * margin), (columns - margin, margin))[side]
        if band == 1:
            total = totals_ref[:, pl.ds(margin + first, height), pl.ds(margin + left, wide)]
        else:
            total = strip_ref[band // 2, :, :, pl.ds(margin + left, wide)]
        if side != 1:
            total = total + from_columns_ref[side // 2, :, pl.ds(first, height), :]
        old = ext_ref[:, pl.ds(margin + first, height), pl.ds(margin + left, wide)]
        new = old + total[:2] / (total[2:] + SPECIMEN_REG)
        out_ref[:, pl.ds(shift_out + first, height), pl.ds(shift_out + left, wide)] = new

    def join(where, piece):
        lanes = pieces[piece]
        start = margin if where == up else rows
        shifts["rows", where, piece].arrived()
        strip_ref[where, :, :, lanes] = (
            totals_ref[:, pl.ds(start, margin), lanes] + from_rows_ref[where, :, :, lanes]
        )

    step()
    renew(1, 1)
    step()
    for side in (0, 1):
        for where in (up, down):
            join(where, side)
            shifts["columns", 2 * where, 1 - side].start()
    step()
    step()
    for where in (up, down):
        join(where, 2)
        renew(2 * where, 1)
        step()
    for band in (1, 0, 2):
        for side in (0, 1):
            shifts["columns", band, side].arrived()
            renew(band, 2 * side)
        step()
    if not last:
        def between():
            step()
            step()

        halo(net, out_ref, margin, between)
    for _ in reducing:
        pass
    whole = whole_ref[...]
    probe_out_ref[...] = probe_ref[...] + whole[:2] / (whole[2:] + PROBE_REG)
    net.finish()


VMEM = pl.BlockSpec(memory_space=pltpu.VMEM)
ROOM = 32 * 1024 * 1024


def first_halo(size, specimen, intensity, margin):
    planes, rows, columns = specimen.shape
    return pl.pallas_call(
        functools.partial(first_halo_kernel, size, margin),
        out_shape=(
            jax.ShapeDtypeStruct((planes, rows + 2 * margin, columns + 2 * margin), jnp.float32),
            jax.ShapeDtypeStruct(intensity.shape, jnp.float32),
        ),
        in_specs=[VMEM] * 4,
        out_specs=(VMEM, VMEM),
        scratch_shapes=[pltpu.SemaphoreType.DMA((8,)), pltpu.SemaphoreType.DMA((8,))],
        compiler_params=pltpu.CompilerParams(
            collective_id=0, has_side_effects=True, vmem_limit_bytes=ROOM
        ),
        name="first_halo",
    )(specimen, intensity, *[jnp.asarray(t) for t in tables(intensity.shape[1])[4:]])


def settle(size, totals, grads, extended, probe_field, margin, last):
    window = probe_field.shape[1]
    wide = extended.shape[2]
    rows, columns = extended.shape[1] - 2 * margin, wide - 2 * margin
    inboxes = []
    height = window
    copies = 20
    for count in size.values():
        for _ in range(int(math.log2(count))):
            if (height // 2) % SUBLANES == 0:
                height //= 2
                inboxes.append(pltpu.VMEM((3, height, window), jnp.float32))
            else:
                inboxes.append(pltpu.VMEM((2, 3, height, window), jnp.float32))
            copies += 2
    out = (2, rows, columns) if last else extended.shape
    return pl.pallas_call(
        functools.partial(settle_kernel, size, margin, last),
        out_shape=(
            jax.ShapeDtypeStruct(out, jnp.float32),
            jax.ShapeDtypeStruct(probe_field.shape, jnp.float32),
        ),
        in_specs=[VMEM] * 4,
        out_specs=(VMEM, VMEM),
        scratch_shapes=[
            pltpu.VMEM((2, 3, margin, wide), jnp.float32),
            pltpu.VMEM((2, 3, margin, wide), jnp.float32),
            pltpu.VMEM((2, 3, rows, margin), jnp.float32),
            pltpu.VMEM(grads.shape, jnp.float32),
            pltpu.VMEM(grads.shape, jnp.float32),
            *inboxes,
            pltpu.SemaphoreType.DMA((copies,)),
            pltpu.SemaphoreType.DMA((copies,)),
        ],
        compiler_params=pltpu.CompilerParams(
            collective_id=2 if last else 1, has_side_effects=True, vmem_limit_bytes=ROOM
        ),
        name="settle_last" if last else "settle",
    )(totals, grads, extended, probe_field)


def body(size, specimen, probe_field, intensity, positions, occupied_slots):
    tile_rows = specimen.shape[1]
    tile_columns = specimen.shape[2]
    window = probe_field.shape[1]
    margin = window // 2
    row_start = lax.axis_index("ty") * tile_rows - margin
    column_start = lax.axis_index("tx") * tile_columns - margin
    corners = positions - jnp.stack([row_start, column_start])[None, :]
    extended, amplitude = first_halo(size, specimen, intensity, margin)
    for iteration in range(ITERS):
        totals, grads = sweep(corners, occupied_slots, extended, probe_field, amplitude)
        extended, probe_field = settle(
            size, totals, grads, extended, probe_field, margin, iteration == ITERS - 1
        )
    return (extended, probe_field)


def solution(mesh):
    return jax.shard_map(
        functools.partial(body, dict(mesh.shape)),
        mesh=mesh,
        in_specs=(
            P(None, "ty", "tx"),
            P(),
            P(("ty", "tx"), None, None),
            P(("ty", "tx"), None),
            P(("ty", "tx")),
        ),
        out_specs=(P(None, "ty", "tx"), P()),
        check_vma=False,
    )
```
